128 devices in a mesh: row: 16 (over y_lo, x, core), col: 8 (over z, y_hi).
Axes of the slice: x: 4, y: 4 (y_hi: 2, y_lo: 2; y = y_hi * 2 + y_lo), z: 4, core: 2. Of those that a mesh axis runs over, the one named last changes fastest.
Arguments:
- amplitudes: float32 [65536, 256], P(None, ('row', 'col')), may hold values from -24 to 24
- integrals: float32 [11264, 65536], P('row', 'col'), may hold values from -0.0234375 to 0.0234375
Outputs:
- ladder: float32 [11264, 256], P('row', 'col')
The draws below stay inside these ranges and needn't reach their ends.
All inputs are finite; a program needn't handle non-finite values.
Results may differ from the reference program's by a relative error of at most 0.00007.
Values sent between devices are 32-bit elements; how exact they have to be, the bound alone decides.
A program may use at most 128 MiB of HBM per device.

```python
import jax
import jax.numpy as jnp
from jax import lax

IJ = 256
CD = 65536
AB = 11264


def with_spikes(values, stream_key, source, target, blocks, factor):
    def block_of(position):
        return (jnp.arange(values.shape[position]) // (values.shape[position] // blocks)).reshape((-1,) + (1,) * (values.ndim - 1 - position))

    one_side = jax.random.permutation(stream_key, blocks)[block_of(target)]
    far = (block_of(target) + blocks // 2) % blocks
    return jnp.where((block_of(source) == one_side) | (block_of(source) == far), factor * values, values)


def block_levels(rng, dims, cuts, smallest, largest):
    factor_of = 1.0
    for axis_at, parts in cuts:
        heights = jax.random.uniform(jax.random.fold_in(jax.random.fold_in(rng, 6), axis_at), (parts,), jnp.float32, smallest / len(cuts), largest / len(cuts))
        factor_of = factor_of * jnp.repeat(jnp.exp(heights), dims[axis_at] // parts).reshape((-1,) + (1,) * (len(dims) - 1 - axis_at))
    return factor_of


def gaussian(rng, extent, deviation, reach, cuts=(), dtype=jnp.bfloat16):
    result = deviation * jax.random.normal(rng, extent, jnp.float32)
    if cuts:
        result = result * block_levels(rng, extent, cuts, -0.22, 0.18)
    return jnp.clip(result, -reach, reach).astype(dtype)


def gaussian_with(rng, dims, spread, reach, split, heavy, held_as=jnp.bfloat16):
    entries = spread * jax.random.normal(rng, dims, jnp.float32)
    if split:
        entries = entries * block_levels(rng, dims, split, -0.22, 0.18)
    return jnp.clip(with_spikes(entries, jax.random.fold_in(rng, 3), *heavy), -reach, reach).astype(held_as)


def setup_inputs(seed: int = 0) -> dict:
    keys = jax.random.split(jax.random.key(seed), 3)
    amplitudes = gaussian_with(keys[0], (CD, IJ), 1.0, 24.0, ((1, 128),), (0, 1, 128, 5.5), jnp.float32)
    integrals = gaussian(keys[1], (AB, CD), CD ** -0.5, 0.0234375, ((0, 16), (1, 8)), jnp.float32)
    return {"amplitudes": amplitudes, "integrals": integrals}


def reference(amplitudes, integrals):
    contracted = jnp.dot(integrals, amplitudes, preferred_element_type=jnp.float32, precision=lax.Precision.HIGHEST)
    return 0.5 * contracted
```

```python
import functools

import jax
import jax.numpy as jnp
from jax import lax
from jax.experimental import pallas as pl
from jax.experimental.pallas import tpu as pltpu
from jax.sharding import PartitionSpec as P

MESH = pl.DeviceIdType.MESH
BF = jnp.bfloat16
F32 = jnp.float32
NT = (((1,), (1,)), ((), ()))

K = 8192
AB = 704
M = 8
CK = K // M
N = 2 * M
TILES = CK // 128
STAGES = 3


def dot(a, b):
    return lax.dot_general(a, b, NT, preferred_element_type=F32)


def split(v):
    hi = v.astype(BF)
    return hi, (v - hi.astype(F32)).astype(BF)


def kernel(amp, integ, out, raw, panel, stage, ah, al, bs, acc, part, land,
           own_sem, a2a_send, a2a_recv, stage_sem, g_send, g_recv, c_recv, rs_send, rs_recv):
    row, col = lax.axis_index("row"), lax.axis_index("col")
    core = lax.rem(row, 2)
    x = lax.rem(row // 2, 4)
    q = row // 8
    z, yhi = col // 2, lax.rem(col, 2)
    cls = lax.rem(q + yhi, 2)

    def rowid(qq, xx, kk):
        return (qq * 4 + xx) * 2 + kk

    xr, xl = lax.rem(x + 1, 4), lax.rem(x + 3, 4)
    xo = lax.rem(x + 2, 4)
    right = (rowid(q, xr, core), col)
    left = (rowid(q, xl, core), col)
    across = (rowid(1 - q, x, core), col)
    sib = (rowid(q, x, 1 - core), col)

    def a2a_dev(step):
        c = lax.rem(col + step, 8)
        return (rowid(lax.rem(cls + lax.rem(c, 2), 2), x, core), c)

    def rs_dev(step):
        return (row, lax.rem(col + step, 8))

    barrier = pltpu.get_barrier_semaphore()

    def greet(dev):
        pl.semaphore_signal(barrier, inc=1, device_id=dev, device_id_type=MESH)

    for dev in (right, left, across, sib):
        greet(dev)
    for s in range(1, 8):
        greet(a2a_dev(s))
    for s in range(1, 8, 2):
        greet(rs_dev(s))
    src_slot = yhi * 4 + z

    def stage_copy(m):
        return pltpu.make_async_copy(integ.at[:, pl.ds(pl.multiple_of(m * CK, CK), CK)],
                                     stage.at[lax.rem(m, STAGES)], stage_sem.at[lax.rem(m, STAGES)])

    own_copies = []
    for m in range(M):
        cp = pltpu.make_async_copy(
            amp.at[pl.ds(pl.multiple_of(col * 2 * K // 128 + m * 2 * TILES, 8), 2 * TILES)],
            raw.at[m, pl.ds(pl.multiple_of(src_slot * 2 * TILES, 8), 2 * TILES)], own_sem.at[m])
        cp.start()
        own_copies.append(cp)
    for m in range(STAGES):
        stage_copy(m).start()
    pl.semaphore_wait(barrier, 15)

    @pl.loop(0, M)
    def _(m):
        for s in range(1, 8):
            c, dev = lax.rem(col + s, 8), a2a_dev(s)
            pltpu.make_async_remote_copy(
                src_ref=amp.at[pl.ds(pl.multiple_of(c * (2 * K // 128) + m * 2 * TILES, 8), 2 * TILES)],
                dst_ref=raw.at[m, pl.ds(pl.multiple_of(src_slot * 2 * TILES, 8), 2 * TILES)],
                send_sem=a2a_send.at[0], recv_sem=a2a_recv.at[m], device_id=dev, device_id_type=MESH,
            ).start()

    acc[...] = jnp.zeros_like(acc)

    def slot(c, xx, kk):
        return (c * 4 + xx) * 2 + kk

    def piece(i, sl, half=None):
        rows = pl.ds(pl.multiple_of(sl * 8, 8), 8)
        if half is None:
            return panel.at[i, rows]
        return panel.at[i, rows, pl.ds(half * (CK // 2), CK // 2)]

    def send(i, sl, dev, sem, half=None):
        ref = piece(i, sl, half)
        pltpu.make_async_remote_copy(src_ref=ref, dst_ref=ref, send_sem=g_send.at[i], recv_sem=sem,
                                     device_id=dev, device_id_type=MESH).start()

    def wait(i, sl, sem):
        ref = piece(i, sl)
        pltpu.make_async_remote_copy(src_ref=ref, dst_ref=ref, send_sem=g_send.at[i], recv_sem=sem,
                                     device_id=right, device_id_type=MESH).wait_recv()

    def share(i, sl):
        send(i, sl, sib, c_recv.at[i])

    own = slot(cls, x, core)

    def first(i):
        m = i
        ref = raw.at[m, pl.ds(0, 7 * 2 * TILES)]

        @pl.when(i < M)
        def _():
            pltpu.make_async_copy(amp.at[pl.ds(0, 2 * TILES)], raw.at[m, pl.ds(0, 2 * TILES)], own_sem.at[m]).wait()
            pltpu.make_async_remote_copy(src_ref=ref, dst_ref=ref, send_sem=a2a_send.at[0], recv_sem=a2a_recv.at[m],
                                         device_id=right, device_id_type=MESH).wait_recv()
            for t in range(TILES):
                for j in range(2):
                    panel[m + j * M, pl.ds(pl.multiple_of(own * 8, 8), 8), t * 128:(t + 1) * 128] = (
                        raw[m, pl.ds(2 * t + j, 8, stride=2 * TILES), :])

        send(i, own, right, g_recv.at[i, 0])
        send(i, own, left, g_recv.at[i, 1])
        send(i, own, across, g_recv.at[i, 2])
        share(i, own)

    def second(i):
        @pl.when(core == 0)
        def _():
            theirs = slot(1 - cls, x, 0)
            wait(i, theirs, g_recv.at[i, 2])
            send(i, theirs, right, g_recv.at[i, 3])
            send(i, theirs, left, g_recv.at[i, 4])
            share(i, theirs)

    def third(i):
        @pl.when(core == 0)
        def _():
            for c, s in ((cls, 0), (1 - cls, 3)):
                wait(i, slot(c, xl, 0), g_recv.at[i, s])
                send(i, slot(c, xl, 0), right, g_recv.at[i, 5 + s // 3], 0)
                share(i, slot(c, xl, 0))
                wait(i, slot(c, xr, 0), g_recv.at[i, s + 1])
                send(i, slot(c, xr, 0), left, g_recv.at[i, 5 + s // 3], 1)
                share(i, slot(c, xr, 0))

        @pl.when(core == 1)
        def _():
            wait(i, slot(cls, xl, 1), g_recv.at[i, 0])
            send(i, slot(cls, xl, 1), right, g_recv.at[i, 3], 0)
            send(i, slot(cls, xl, 1), across, g_recv.at[i, 4])
            share(i, slot(cls, xl, 1))
            wait(i, slot(cls, xr, 1), g_recv.at[i, 1])
            send(i, slot(cls, xr, 1), left, g_recv.at[i, 3], 1)
            send(i, slot(cls, xr, 1), across, g_recv.at[i, 5])
            share(i, slot(cls, xr, 1))

    def fourth(i):
        @pl.when(core == 0)
        def _():
            for c, s in ((cls, 5), (1 - cls, 6)):
                wait(i, slot(c, xo, 0), g_recv.at[i, s])
                share(i, slot(c, xo, 0))

        @pl.when(core == 1)
        def _():
            wait(i, slot(cls, xo, 1), g_recv.at[i, 3])
            send(i, slot(cls, xo, 1), across, g_recv.at[i, 6])
            share(i, slot(cls, xo, 1))
            for xx, s in ((x, 2), (xl, 4), (xr, 5)):
                wait(i, slot(1 - cls, xx, 1), g_recv.at[i, s])
                share(i, slot(1 - cls, xx, 1))

    def fifth(i):
        @pl.when(core == 1)
        def _():
            wait(i, slot(1 - cls, xo, 1), g_recv.at[i, 6])
            share(i, slot(1 - cls, xo, 1))

    def convert(m):
        st = lax.rem(m, STAGES)
        stage_copy(m).wait()

        @pl.loop(0, AB // 16, unroll=2)
        def _(r):
            rows = pl.ds(pl.multiple_of(r * 16, 16), 16)
            hi, lo = split(stage[st, rows, :])
            ah[m, rows, :] = hi
            al[m, rows, :] = lo

        @pl.when(m + STAGES < M)
        def _():
            stage_copy(m + STAGES).start()

    def compute(i):
        m = lax.rem(i, M)
        ref = panel.at[i, pl.ds(0, 64)]
        pltpu.make_async_remote_copy(src_ref=ref, dst_ref=ref, send_sem=g_send.at[i], recv_sem=c_recv.at[i],
                                     device_id=sib, device_id_type=MESH).wait_recv()
        mask = lax.rem(lax.broadcasted_iota(jnp.int32, (16, CK), 0), 8) < 4
        for xx in range(4):
            v0 = panel[i, xx * 16:xx * 16 + 16, :]
            v1 = panel[i, 64 + xx * 16:64 + xx * 16 + 16, :]
            for y, v in ((0, jnp.where(mask, v0, v1)), (1, jnp.where(mask, v1, v0))):
                hi, lo = split(v)
                at = y * 64 + xx * 16
                bs[at:at + 16, :] = hi
                bs[128 + at:128 + at + 16, :] = lo
        for a0, a1 in ((0, 352), (352, 704)):
            acc[a0:a1, :] += dot(ah[m, a0:a1, :], bs[...])
            acc[a0:a1, 0:128] += dot(al[m, a0:a1, :], bs[0:128, :])

    def finish(h):
        part[h, :, :] = (acc[:, 0:128] + acc[:, 128:256]).T
        acc[...] = jnp.zeros_like(acc)
        for s in range(1, 8):
            c = lax.rem(col + s, 8)
            pltpu.make_async_remote_copy(
                src_ref=part.at[h, pl.ds(pl.multiple_of(c * 16, 16), 16)], dst_ref=land.at[h, col],
                send_sem=rs_send.at[h], recv_sem=rs_recv.at[h], device_id=rs_dev(s), device_id_type=MESH).start()
        land[h, col, :, :] = part[h, pl.ds(pl.multiple_of(col * 16, 16), 16), :]

    LAG = 5

    @pl.loop(0, N + LAG)
    def _(i):
        @pl.when(i < N)
        def _():
            first(i)

        @pl.when((i >= 1) & (i < N + 1))
        def _():
            second(i - 1)

        @pl.when((i >= 2) & (i < N + 2))
        def _():
            third(i - 2)

        @pl.when((i >= 3) & (i < N + 3))
        def _():
            fourth(i - 3)

        @pl.when((i >= 4) & (i < N + 4))
        def _():
            fifth(i - 4)

        @pl.when(i < M)
        def _():
            convert(i)

        @pl.when(i >= LAG)
        def _():
            compute(i - LAG)

        @pl.when(i == M - 1 + LAG)
        def _():
            finish(0)

        @pl.when(i == N - 1 + LAG)
        def _():
            finish(1)

    for h in range(2):
        ref = land.at[h, pl.ds(0, 7)]
        pltpu.make_async_remote_copy(src_ref=ref, dst_ref=ref, send_sem=rs_send.at[h], recv_sem=rs_recv.at[h],
                                     device_id=right, device_id_type=MESH).wait_recv()
        total = land[h, 0]
        for c in range(1, 8):
            total += land[h, c]
        total = 0.5 * total
        for kk in range(2):
            for yy in range(2):
                for zz in range(4):
                    r = kk * 16 + zz * 4 + yy * 2 + h
                    s = kk * 8 + yy * 4 + zz
                    out[r:r + 1, :] = total[s:s + 1, :]

    ref = raw.at[pl.ds(0, 7)]
    pltpu.make_async_remote_copy(src_ref=ref, dst_ref=ref, send_sem=a2a_send.at[0], recv_sem=a2a_recv.at[0],
                                 device_id=right, device_id_type=MESH).wait_send()

    @pl.loop(0, N)
    def _(i):
        ref = panel.at[i, pl.ds(0, 120)]
        pltpu.make_async_remote_copy(src_ref=ref, dst_ref=ref, send_sem=g_send.at[i], recv_sem=c_recv.at[i],
                                     device_id=right, device_id_type=MESH).wait_send()

    for h in range(2):
        ref = land.at[h, pl.ds(0, 7)]
        pltpu.make_async_remote_copy(src_ref=ref, dst_ref=ref, send_sem=rs_send.at[h], recv_sem=rs_recv.at[h],
                                     device_id=right, device_id_type=MESH).wait_send()


def per_device(amplitudes, integrals):
    amp = amplitudes.reshape(512, 128, 2).transpose(0, 2, 1).reshape(1024, 128)
    dma = pltpu.SemaphoreType.DMA
    out = pl.pallas_call(
        kernel,
        out_shape=jax.ShapeDtypeStruct((32, AB), F32),
        in_specs=[pl.BlockSpec(memory_space=pl.ANY)] * 2,
        out_specs=pl.BlockSpec(memory_space=pltpu.VMEM),
        scratch_shapes=[
            pltpu.VMEM((M, 8 * 2 * TILES, 128), F32),
            pltpu.VMEM((N, 128, CK), F32),
            pltpu.VMEM((STAGES, AB, CK), F32),
            pltpu.VMEM((M, AB, CK), BF),
            pltpu.VMEM((M, AB, CK), BF),
            pltpu.VMEM((256, CK), BF),
            pltpu.VMEM((AB, 256), F32),
            pltpu.VMEM((2, 128, AB), F32),
            pltpu.VMEM((2, 8, 16, AB), F32),
            dma((M,)), dma((1,)), dma((M,)), dma((STAGES,)),
            dma((N,)), dma((N, 7)), dma((N,)), dma((2,)), dma((2,)),
        ],
        compiler_params=pltpu.CompilerParams(collective_id=0, has_side_effects=True, vmem_limit_bytes=60 * 2**20),
        cost_estimate=pl.CostEstimate(flops=2 * AB * K * 256, bytes_accessed=4 * AB * K, transcendentals=0),
    )(amp, integrals)
    return out.T


def solution(mesh):
    return jax.shard_map(
        per_device,
        mesh=mesh,
        in_specs=(P(None, ("row", "col")), P("row", "col")),
        out_specs=P("row", "col"),
        check_vma=False,
    )
```

```python
import functools

import jax
import jax.numpy as jnp
from jax import lax
from jax.experimental import pallas as pl
from jax.experimental.pallas import tpu as pltpu
from jax.sharding import PartitionSpec as P

MESH = pl.DeviceIdType.MESH
BF = jnp.bfloat16
F32 = jnp.float32
NT = (((1,), (1,)), ((), ()))

K = 8192
AB = 704
M = 8
CK = K // M
N = 2 * M
TILES = CK // 128
STAGES = 3
LAGS = (3, 6, 9, 12, 13)
EVERY = 99


def dot(a, b):
    return lax.dot_general(a, b, NT, preferred_element_type=F32)


def split(v):
    hi = v.astype(BF)
    return hi, (v - hi.astype(F32)).astype(BF)


def kernel(amp, integ, out, raw, panel, stage, ah, al, bs, acc, part, land,
           own_sem, a2a_send, a2a_recv, stage_sem, g_send, g_recv, c_recv, rs_send, rs_recv):
    row, col = lax.axis_index("row"), lax.axis_index("col")
    core = lax.rem(row, 2)
    x = lax.rem(row // 2, 4)
    q = row // 8
    z, yhi = col // 2, lax.rem(col, 2)
    cls = lax.rem(q + yhi, 2)

    def rowid(qq, xx, kk):
        return (qq * 4 + xx) * 2 + kk

    xr, xl = lax.rem(x + 1, 4), lax.rem(x + 3, 4)
    xo = lax.rem(x + 2, 4)
    right = (rowid(q, xr, core), col)
    left = (rowid(q, xl, core), col)
    across = (rowid(1 - q, x, core), col)
    sib = (rowid(q, x, 1 - core), col)

    def a2a_dev(step):
        c = partner(step)
        return (rowid(lax.rem(cls + lax.rem(c, 2), 2), x, core), c)

    FAR_FIRST = (5, 3, 7, 1, 4, 2, 6)

    def partner(step):
        return lax.rem(z + step // 2, 4) * 2 + lax.rem(yhi + step, 2)

    def rs_dev(step):
        return (row, partner(step))

    barrier = pltpu.get_barrier_semaphore()

    def greet(dev):
        pl.semaphore_signal(barrier, inc=1, device_id=dev, device_id_type=MESH)

    for dev in (right, left, across, sib):
        greet(dev)
    for s in range(1, 8):
        greet(a2a_dev(s))
    for s in range(1, 8, 2):
        greet(rs_dev(s))
    src_slot = yhi * 4 + z

    def stage_copy(m):
        return pltpu.make_async_copy(integ.at[:, pl.ds(pl.multiple_of(m * CK, CK), CK)],
                                     stage.at[lax.rem(m, STAGES)], stage_sem.at[lax.rem(m, STAGES)])

    own_copies = []
    for m in range(M):
        cp = pltpu.make_async_copy(
            amp.at[pl.ds(pl.multiple_of(col * 2 * K // 128 + m * 2 * TILES, 8), 2 * TILES)],
            raw.at[m, pl.ds(pl.multiple_of(src_slot * 2 * TILES, 8), 2 * TILES)], own_sem.at[m])
        cp.start()
        own_copies.append(cp)
    for m in range(STAGES):
        stage_copy(m).start()
    pl.semaphore_wait(barrier, 15)

    @pl.loop(0, M)
    def _(m):
        for s in FAR_FIRST:
            c, dev = partner(s), a2a_dev(s)
            pltpu.make_async_remote_copy(
                src_ref=amp.at[pl.ds(pl.multiple_of(c * (2 * K // 128) + m * 2 * TILES, 8), 2 * TILES)],
                dst_ref=raw.at[m, pl.ds(pl.multiple_of(src_slot * 2 * TILES, 8), 2 * TILES)],
                send_sem=a2a_send.at[0], recv_sem=a2a_recv.at[m], device_id=dev, device_id_type=MESH,
            ).start()

    acc[...] = jnp.zeros_like(acc)

    def slot(c, xx, kk):
        return (c * 4 + xx) * 2 + kk

    def piece(i, sl, half=None):
        rows = pl.ds(pl.multiple_of(sl * 8, 8), 8)
        if half is None:
            return panel.at[i, rows]
        return panel.at[i, rows, pl.ds(half * (CK // 2), CK // 2)]

    def send(i, sl, dev, sem, half=None):
        ref = piece(i, sl, half)
        pltpu.make_async_remote_copy(src_ref=ref, dst_ref=ref, send_sem=g_send.at[i], recv_sem=sem,
                                     device_id=dev, device_id_type=MESH).start()

    def wait(i, sl, sem):
        ref = piece(i, sl)
        pltpu.make_async_remote_copy(src_ref=ref, dst_ref=ref, send_sem=g_send.at[i], recv_sem=sem,
                                     device_id=right, device_id_type=MESH).wait_recv()

    def share(i, sl):
        send(i, sl, sib, c_recv.at[i])

    own = slot(cls, x, core)

    def y_first(i):
        return (core == 0) | (lax.rem(i, EVERY) == EVERY - 1)

    def x_first(i):
        return (core == 1) & (lax.rem(i, EVERY) != EVERY - 1)

    def first(i):
        m = i
        ref = raw.at[m, pl.ds(0, 7 * 2 * TILES)]

        @pl.when(i < M)
        def _():
            pltpu.make_async_copy(amp.at[pl.ds(0, 2 * TILES)], raw.at[m, pl.ds(0, 2 * TILES)], own_sem.at[m]).wait()
            pltpu.make_async_remote_copy(src_ref=ref, dst_ref=ref, send_sem=a2a_send.at[0], recv_sem=a2a_recv.at[m],
                                         device_id=right, device_id_type=MESH).wait_recv()
            for t in range(TILES):
                for j in range(2):
                    panel[m + j * M, pl.ds(pl.multiple_of(own * 8, 8), 8), t * 128:(t + 1) * 128] = (
                        raw[m, pl.ds(2 * t + j, 8, stride=2 * TILES), :])

        send(i, own, right, g_recv.at[i, 0])
        send(i, own, left, g_recv.at[i, 1])
        send(i, own, across, g_recv.at[i, 2])
        share(i, own)

    def second(i):
        @pl.when(y_first(i))
        def _():
            theirs = slot(1 - cls, x, core)
            wait(i, theirs, g_recv.at[i, 2])
            send(i, theirs, right, g_recv.at[i, 3])
            send(i, theirs, left, g_recv.at[i, 4])
            share(i, theirs)

    def third(i):
        @pl.when(y_first(i))
        def _():
            for c, s in ((cls, 0), (1 - cls, 3)):
                wait(i, slot(c, xl, core), g_recv.at[i, s])
                send(i, slot(c, xl, core), right, g_recv.at[i, 5 + s // 3], 0)
                share(i, slot(c, xl, core))
                wait(i, slot(c, xr, core), g_recv.at[i, s + 1])
                send(i, slot(c, xr, core), left, g_recv.at[i, 5 + s // 3], 1)
                share(i, slot(c, xr, core))

        @pl.when(x_first(i))
        def _():
            wait(i, slot(cls, xl, core), g_recv.at[i, 0])
            send(i, slot(cls, xl, core), right, g_recv.at[i, 3], 0)
            send(i, slot(cls, xl, core), across, g_recv.at[i, 4])
            share(i, slot(cls, xl, core))
            wait(i, slot(cls, xr, core), g_recv.at[i, 1])
            send(i, slot(cls, xr, core), left, g_recv.at[i, 3], 1)
            send(i, slot(cls, xr, core), across, g_recv.at[i, 5])
            share(i, slot(cls, xr, core))

    def fourth(i):
        @pl.when(y_first(i))
        def _():
            for c, s in ((cls, 5), (1 - cls, 6)):
                wait(i, slot(c, xo, core), g_recv.at[i, s])
                share(i, slot(c, xo, core))

        @pl.when(x_first(i))
        def _():
            wait(i, slot(cls, xo, core), g_recv.at[i, 3])
            send(i, slot(cls, xo, core), across, g_recv.at[i, 6])
            share(i, slot(cls, xo, core))
            for xx, s in ((x, 2), (xl, 4), (xr, 5)):
                wait(i, slot(1 - cls, xx, core), g_recv.at[i, s])
                share(i, slot(1 - cls, xx, core))

    def fifth(i):
        @pl.when(x_first(i))
        def _():
            wait(i, slot(1 - cls, xo, core), g_recv.at[i, 6])
            share(i, slot(1 - cls, xo, core))

    def convert(m):
        st = lax.rem(m, STAGES)
        stage_copy(m).wait()

        @pl.loop(0, AB // 16, unroll=2)
        def _(r):
            rows = pl.ds(pl.multiple_of(r * 16, 16), 16)
            hi, lo = split(stage[st, rows, :])
            ah[m, rows, :] = hi
            al[m, rows, :] = lo

        @pl.when(m + STAGES < M)
        def _():
            stage_copy(m + STAGES).start()

    def compute(i):
        m = lax.rem(i, M)
        ref = panel.at[i, pl.ds(0, 64)]
        pltpu.make_async_remote_copy(src_ref=ref, dst_ref=ref, send_sem=g_send.at[i], recv_sem=c_recv.at[i],
                                     device_id=sib, device_id_type=MESH).wait_recv()
        mask = lax.rem(lax.broadcasted_iota(jnp.int32, (16, CK), 0), 8) < 4
        for xx in range(4):
            v0 = panel[i, xx * 16:xx * 16 + 16, :]
            v1 = panel[i, 64 + xx * 16:64 + xx * 16 + 16, :]
            for y, v in ((0, jnp.where(mask, v0, v1)), (1, jnp.where(mask, v1, v0))):
                hi, lo = split(v)
                at = y * 64 + xx * 16
                bs[at:at + 16, :] = hi
                bs[128 + at:128 + at + 16, :] = lo
        for a0, a1 in ((0, 352), (352, 704)):
            acc[a0:a1, :] += dot(ah[m, a0:a1, :], bs[...])
            acc[a0:a1, 0:128] += dot(al[m, a0:a1, :], bs[0:128, :])

    def finish(h):
        part[h, :, :] = (acc[:, 0:128] + acc[:, 128:256]).T
        acc[...] = jnp.zeros_like(acc)
        for s in FAR_FIRST:
            c = partner(s)
            pltpu.make_async_remote_copy(
                src_ref=part.at[h, pl.ds(pl.multiple_of(c * 16, 16), 16)], dst_ref=land.at[h, col],
                send_sem=rs_send.at[h], recv_sem=rs_recv.at[h], device_id=rs_dev(s), device_id_type=MESH).start()
        land[h, col, :, :] = part[h, pl.ds(pl.multiple_of(col * 16, 16), 16), :]

    def at(i, lag, f):
        @pl.when((i >= lag) & (i < N + lag))
        def _():
            f(i - lag)

    L2, L3, L4, L5, LC = LAGS

    @pl.loop(0, N + LC)
    def _(i):
        at(i, 0, first)
        at(i, L2, second)
        at(i, L3, third)
        at(i, L4, fourth)
        at(i, L5, fifth)

        @pl.when(i < M)
        def _():
            convert(i)

        at(i, LC, compute)

        @pl.when(i == M - 1 + LC)
        def _():
            finish(0)

        @pl.when(i == N - 1 + LC)
        def _():
            finish(1)

    for h in range(2):
        ref = land.at[h, pl.ds(0, 7)]
        pltpu.make_async_remote_copy(src_ref=ref, dst_ref=ref, send_sem=rs_send.at[h], recv_sem=rs_recv.at[h],
                                     device_id=right, device_id_type=MESH).wait_recv()
        total = land[h, 0]
        for c in range(1, 8):
            total += land[h, c]
        total = 0.5 * total
        for kk in range(2):
            for yy in range(2):
                for zz in range(4):
                    r = kk * 16 + zz * 4 + yy * 2 + h
                    s = kk * 8 + yy * 4 + zz
                    out[r:r + 1, :] = total[s:s + 1, :]

    ref = raw.at[pl.ds(0, 7)]
    pltpu.make_async_remote_copy(src_ref=ref, dst_ref=ref, send_sem=a2a_send.at[0], recv_sem=a2a_recv.at[0],
                                 device_id=right, device_id_type=MESH).wait_send()

    @pl.loop(0, N)
    def _(i):
        ref = panel.at[i, pl.ds(0, 120)]
        pltpu.make_async_remote_copy(src_ref=ref, dst_ref=ref, send_sem=g_send.at[i], recv_sem=c_recv.at[i],
                                     device_id=right, device_id_type=MESH).wait_send()

    for h in range(2):
        ref = land.at[h, pl.ds(0, 7)]
        pltpu.make_async_remote_copy(src_ref=ref, dst_ref=ref, send_sem=rs_send.at[h], recv_sem=rs_recv.at[h],
                                     device_id=right, device_id_type=MESH).wait_send()


def per_device(amplitudes, integrals):
    amp = amplitudes.reshape(512, 128, 2).transpose(0, 2, 1).reshape(1024, 128)
    dma = pltpu.SemaphoreType.DMA
    out = pl.pallas_call(
        kernel,
        out_shape=jax.ShapeDtypeStruct((32, AB), F32),
        in_specs=[pl.BlockSpec(memory_space=pl.ANY)] * 2,
        out_specs=pl.BlockSpec(memory_space=pltpu.VMEM),
        scratch_shapes=[
            pltpu.VMEM((M, 8 * 2 * TILES, 128), F32),
            pltpu.VMEM((N, 128, CK), F32),
            pltpu.VMEM((STAGES, AB, CK), F32),
            pltpu.VMEM((M, AB, CK), BF),
            pltpu.VMEM((M, AB, CK), BF),
            pltpu.VMEM((256, CK), BF),
            pltpu.VMEM((AB, 256), F32),
            pltpu.VMEM((2, 128, AB), F32),
            pltpu.VMEM((2, 8, 16, AB), F32),
            dma((M,)), dma((1,)), dma((M,)), dma((STAGES,)),
            dma((N,)), dma((N, 7)), dma((N,)), dma((2,)), dma((2,)),
        ],
        compiler_params=pltpu.CompilerParams(collective_id=0, has_side_effects=True, vmem_limit_bytes=60 * 2**20),
        cost_estimate=pl.CostEstimate(flops=2 * AB * K * 256, bytes_accessed=4 * AB * K, transcendentals=0),
    )(amp, integrals)
    return out.T


def solution(mesh):
    return jax.shard_map(
        per_device,
        mesh=mesh,
        in_specs=(P(None, ("row", "col")), P("row", "col")),
        out_specs=P("row", "col"),
        check_vma=False,
    )
```

```python
import functools

import jax
import jax.numpy as jnp
from jax import lax
from jax.experimental import pallas as pl
from jax.experimental.pallas import tpu as pltpu
from jax.sharding import PartitionSpec as P

MESH = pl.DeviceIdType.MESH
BF = jnp.bfloat16
F32 = jnp.float32
NT = (((1,), (1,)), ((), ()))

K = 8192
AB = 704
M = 8
CK = K // M
N = 2 * M
TILES = CK // 128
GROUPS = tuple((m, 1) for m in range(M))
PRE = 0
STAGES = 6
LAG = dict(y=3.1, xa=6.2, xb=6.3, oa=9.2, ob=9.3, x=6.2, o=9.2, y3=12.3, compute=13)
EVERY = 99


def dot(a, b):
    return lax.dot_general(a, b, NT, preferred_element_type=F32)


def split(v):
    hi = v.astype(BF)
    return hi, (v - hi.astype(F32)).astype(BF)


def kernel(amp, integ, out, raw, panel, stage, ah, al, bs, acc, part, land,
           own_sem, a2a_send, a2a_recv, stage_sem, g_send, g_recv, c_recv, rs_send, rs_recv):
    row, col = lax.axis_index("row"), lax.axis_index("col")
    core = lax.rem(row, 2)
    x = lax.rem(row // 2, 4)
    q = row // 8
    z, yhi = col // 2, lax.rem(col, 2)
    cls = lax.rem(q + yhi, 2)

    def rowid(qq, xx, kk):
        return (qq * 4 + xx) * 2 + kk

    xr, xl = lax.rem(x + 1, 4), lax.rem(x + 3, 4)
    xo = lax.rem(x + 2, 4)
    right = (rowid(q, xr, core), col)
    left = (rowid(q, xl, core), col)
    across = (rowid(1 - q, x, core), col)
    sib = (rowid(q, x, 1 - core), col)

    def a2a_dev(step):
        c = partner(step)
        return (rowid(lax.rem(cls + lax.rem(c, 2), 2), x, core), c)

    FAR_FIRST = (5, 3, 7, 1, 4, 2, 6)

    def partner(step):
        return lax.rem(z + step // 2, 4) * 2 + lax.rem(yhi + step, 2)

    def rs_dev(step):
        return (row, partner(step))

    barrier = pltpu.get_barrier_semaphore()

    def greet(dev):
        pl.semaphore_signal(barrier, inc=1, device_id=dev, device_id_type=MESH)

    for dev in (right, left, across, sib):
        greet(dev)
    for s in range(1, 8):
        greet(a2a_dev(s))
    src_slot = yhi * 4 + z

    def stage_copy(m):
        return pltpu.make_async_copy(integ.at[:, pl.ds(pl.multiple_of(m * CK, CK), CK)],
                                     stage.at[lax.rem(m, STAGES)], stage_sem.at[lax.rem(m, STAGES)])

    own_rows = pl.ds(pl.multiple_of(src_slot * 2 * TILES, 8), 2 * TILES)
    own_copy = pltpu.make_async_copy(amp.at[col], raw.at[:, own_rows], own_sem.at[0])
    own_copy.start()
    for m in range(STAGES):
        stage_copy(m).start()
    def convert(m):
        st = lax.rem(m, STAGES)
        stage_copy(m).wait()

        @pl.loop(0, AB // 16, unroll=2)
        def _(r):
            rows = pl.ds(pl.multiple_of(r * 16, 16), 16)
            hi, lo = split(stage[st, rows, :])
            ah[m, rows, :] = hi
            al[m, rows, :] = lo

        @pl.when(m + STAGES < M)
        def _():
            stage_copy(m + STAGES).start()

    pl.semaphore_wait(barrier, 11)

    for g, (m, n) in enumerate(GROUPS):
        for s in FAR_FIRST:
            pltpu.make_async_remote_copy(
                src_ref=amp.at[partner(s), pl.ds(m, n)], dst_ref=raw.at[pl.ds(m, n), own_rows],
                send_sem=a2a_send.at[0], recv_sem=a2a_recv.at[g], device_id=a2a_dev(s), device_id_type=MESH,
            ).start()

    acc[...] = jnp.zeros_like(acc)
    for m in range(PRE):
        convert(m)
    own_copy.wait()

    def slot(c, xx, kk):
        return (kk * 2 + c) * 4 + xx

    def piece(i, sl, half=None):
        rows = pl.ds(pl.multiple_of(sl * 8, 8), 8)
        if half is None:
            return panel.at[i, rows]
        return panel.at[i, rows, pl.ds(half * (CK // 2), CK // 2)]

    def send(i, sl, dev, sem, half=None):
        ref = piece(i, sl, half)
        pltpu.make_async_remote_copy(src_ref=ref, dst_ref=ref, send_sem=g_send.at[i], recv_sem=sem,
                                     device_id=dev, device_id_type=MESH).start()

    def wait(i, sl, sem):
        ref = piece(i, sl)
        pltpu.make_async_remote_copy(src_ref=ref, dst_ref=ref, send_sem=g_send.at[i], recv_sem=sem,
                                     device_id=right, device_id_type=MESH).wait_recv()

    def share(i, c):
        ref = panel.at[i, pl.ds(pl.multiple_of(slot(c, 0, core) * 8, 8), 32)]
        pltpu.make_async_remote_copy(src_ref=ref, dst_ref=ref, send_sem=g_send.at[i], recv_sem=c_recv.at[i],
                                     device_id=sib, device_id_type=MESH).start()

    own = slot(cls, x, core)

    def y_first(i):
        return (core == 0) | (lax.rem(i, EVERY) == EVERY - 1)

    def x_first(i):
        return (core == 1) & (lax.rem(i, EVERY) != EVERY - 1)

    def first(i):
        m = i
        for g, (m0, n) in enumerate(GROUPS):
            @pl.when(i == m0)
            def _():
                ref = raw.at[pl.ds(m0, n), pl.ds(0, 7 * 2 * TILES)]
                pltpu.make_async_remote_copy(src_ref=ref, dst_ref=ref, send_sem=a2a_send.at[0], recv_sem=a2a_recv.at[g],
                                             device_id=right, device_id_type=MESH).wait_recv()

        @pl.when(i < M)
        def _():
            for t in range(TILES):
                for j in range(2):
                    panel[m + j * M, pl.ds(pl.multiple_of(own * 8, 8), 8), t * 128:(t + 1) * 128] = (
                        raw[m, pl.ds(2 * t + j, 8, stride=2 * TILES), :])

        send(i, own, right, g_recv.at[i, 0])
        send(i, own, left, g_recv.at[i, 1])
        send(i, own, across, g_recv.at[i, 2])

    def from_sides(i, c, s, fwd, on_across):
        for xx, dev, k in ((xl, right, 0), (xr, left, 1)):
            wait(i, slot(c, xx, core), g_recv.at[i, s + k])
            send(i, slot(c, xx, core), dev, g_recv.at[i, fwd], k)
            if on_across:
                send(i, slot(c, xx, core), across, g_recv.at[i, 4 + k])

    def y_theirs(i):
        theirs = slot(1 - cls, x, core)
        wait(i, theirs, g_recv.at[i, 2])
        send(i, theirs, right, g_recv.at[i, 3])
        send(i, theirs, left, g_recv.at[i, 4])

    def y_sides_own(i):
        from_sides(i, cls, 0, 5, False)

    def y_sides_theirs(i):
        from_sides(i, 1 - cls, 3, 6, False)

    def y_far_own(i):
        wait(i, slot(cls, xo, core), g_recv.at[i, 5])
        share(i, cls)

    def y_far_theirs(i):
        wait(i, slot(1 - cls, xo, core), g_recv.at[i, 6])
        share(i, 1 - cls)

    def x_sides(i):
        from_sides(i, cls, 0, 3, True)

    def x_far(i):
        wait(i, slot(cls, xo, core), g_recv.at[i, 3])
        send(i, slot(cls, xo, core), across, g_recv.at[i, 6])
        share(i, cls)

    def x_theirs(i):
        for xx, k in ((x, 2), (xl, 4), (xr, 5), (xo, 6)):
            wait(i, slot(1 - cls, xx, core), g_recv.at[i, k])
        share(i, 1 - cls)

    def compute(i):
        m = lax.rem(i, M)
        ref = panel.at[i, pl.ds(0, 64)]
        pltpu.make_async_remote_copy(src_ref=ref, dst_ref=ref, send_sem=g_send.at[i], recv_sem=c_recv.at[i],
                                     device_id=sib, device_id_type=MESH).wait_recv()
        mask = lax.rem(lax.broadcasted_iota(jnp.int32, (16, CK), 0), 8) < 4
        for xx in range(4):
            v0, v1 = (jnp.concatenate([panel[i, slot(c, xx, kk) * 8:slot(c, xx, kk) * 8 + 8, :] for kk in range(2)], 0)
                      for c in range(2))
            for y, v in ((0, jnp.where(mask, v0, v1)), (1, jnp.where(mask, v1, v0))):
                hi, lo = split(v)
                at = y * 64 + xx * 16
                bs[at:at + 16, :] = hi
                bs[128 + at:128 + at + 16, :] = lo
        for a0, a1 in ((0, 704),):
            acc[a0:a1, :] += dot(ah[m, a0:a1, :], bs[...])
            acc[a0:a1, 0:128] += dot(al[m, a0:a1, :], bs[0:128, :])

    def finish(h, _):
        part[h, :, :] = (acc[:, 0:128] + acc[:, 128:256]).T
        for s in FAR_FIRST:
            c = partner(s)
            pltpu.make_async_remote_copy(
                src_ref=part.at[h, pl.ds(pl.multiple_of(c * 16, 16), 16)], dst_ref=land.at[h, col],
                send_sem=rs_send.at[h], recv_sem=rs_recv.at[h], device_id=rs_dev(s), device_id_type=MESH).start()
        land[h, col, :, :] = part[h, pl.ds(pl.multiple_of(col * 16, 16), 16), :]
        if h == 0:
            acc[...] = jnp.zeros_like(acc)

    always = lambda i: True
    work = sorted([
        (0.0, first, always), (LAG["y"], y_theirs, y_first), (LAG["xa"], y_sides_own, y_first),
        (LAG["xb"], y_sides_theirs, y_first), (LAG["oa"], y_far_own, y_first), (LAG["ob"], y_far_theirs, y_first),
        (LAG["x"], x_sides, x_first), (LAG["o"], x_far, x_first), (LAG["y3"], x_theirs, x_first),
    ], key=lambda item: item[0] % 1)
    LC = int(LAG["compute"])

    def at(step, lag, f, role):
        i = step - lag

        @pl.when((i >= 0) & (i < N) & role(i))
        def _():
            f(i)

    @pl.loop(0, N + LC)
    def _(step):
        for lag, f, role in work:
            at(step, int(lag), f, role)

        @pl.when(step < M)
        def _():
            convert(step)

        at(step, LC, compute, always)
        for h in range(2):
            at(step, LC, functools.partial(finish, h), lambda i: i == h * M + M - 1)

    for h in range(2):
        ref = land.at[h, pl.ds(0, 7)]
        pltpu.make_async_remote_copy(src_ref=ref, dst_ref=ref, send_sem=rs_send.at[h], recv_sem=rs_recv.at[h],
                                     device_id=right, device_id_type=MESH).wait_recv()
        total = land[h, 0]
        for c in range(1, 8):
            total += land[h, c]
        total = 0.5 * total
        for kk in range(2):
            for yy in range(2):
                for zz in range(4):
                    r = kk * 16 + zz * 4 + yy * 2 + h
                    s = kk * 8 + yy * 4 + zz
                    out[r:r + 1, :] = total[s:s + 1, :]

    ref = raw.at[:, pl.ds(0, 7 * 2 * TILES)]
    pltpu.make_async_remote_copy(src_ref=ref, dst_ref=ref, send_sem=a2a_send.at[0], recv_sem=a2a_recv.at[0],
                                 device_id=right, device_id_type=MESH).wait_send()

    @pl.loop(0, N)
    def _(i):
        ref = panel.at[i, pl.ds(0, 120)]
        pltpu.make_async_remote_copy(src_ref=ref, dst_ref=ref, send_sem=g_send.at[i], recv_sem=c_recv.at[i],
                                     device_id=right, device_id_type=MESH).wait_send()

    for h in range(2):
        ref = land.at[h, pl.ds(0, 7)]
        pltpu.make_async_remote_copy(src_ref=ref, dst_ref=ref, send_sem=rs_send.at[h], recv_sem=rs_recv.at[h],
                                     device_id=right, device_id_type=MESH).wait_send()


def per_device(amplitudes, integrals):
    amp = amplitudes.reshape(512, 128, 2).transpose(0, 2, 1).reshape(8, M, 2 * TILES, 128)
    dma = pltpu.SemaphoreType.DMA
    out = pl.pallas_call(
        kernel,
        out_shape=jax.ShapeDtypeStruct((32, AB), F32),
        in_specs=[pl.BlockSpec(memory_space=pl.ANY)] * 2,
        out_specs=pl.BlockSpec(memory_space=pltpu.VMEM),
        scratch_shapes=[
            pltpu.VMEM((M, 8 * 2 * TILES, 128), F32),
            pltpu.VMEM((N, 128, CK), F32),
            pltpu.VMEM((STAGES, AB, CK), F32),
            pltpu.VMEM((M, AB, CK), BF),
            pltpu.VMEM((M, AB, CK), BF),
            pltpu.VMEM((256, CK), BF),
            pltpu.VMEM((AB, 256), F32),
            pltpu.VMEM((2, 128, AB), F32),
            pltpu.VMEM((2, 8, 16, AB), F32),
            dma((1,)), dma((1,)), dma((len(GROUPS),)), dma((STAGES,)),
            dma((N,)), dma((N, 7)), dma((N,)), dma((2,)), dma((2,)),
        ],
        compiler_params=pltpu.CompilerParams(collective_id=0, has_side_effects=True, vmem_limit_bytes=60 * 2**20),
        cost_estimate=pl.CostEstimate(flops=2 * AB * K * 256, bytes_accessed=4 * AB * K, transcendentals=0),
    )(amp, integrals)
    return out.T


def solution(mesh):
    return jax.shard_map(
        per_device,
        mesh=mesh,
        in_specs=(P(None, ("row", "col")), P("row", "col")),
        out_specs=P("row", "col"),
        check_vma=False,
    )
```

```python
import functools

import jax
import jax.numpy as jnp
from jax import lax
from jax.experimental import pallas as pl
from jax.experimental.pallas import tpu as pltpu
from jax.sharding import PartitionSpec as P

MESH = pl.DeviceIdType.MESH
BF = jnp.bfloat16
F32 = jnp.float32
NT = (((1,), (1,)), ((), ()))

K = 8192
AB = 704
M = 8
CK = K // M
N = 2 * M
TILES = CK // 128
GROUPS = tuple((m, 1) for m in range(M))
PRE = 0
STAGES = 6
LAG = dict(y=3.1, xa=6.2, xb=6.3, oa=9.2, ob=9.3, x=6.2, o=9.2, y3=12.3, compute=13)
EVERY = 99


def dot(a, b):
    return lax.dot_general(a, b, NT, preferred_element_type=F32)


def split(v):
    hi = v.astype(BF)
    return hi, (v - hi.astype(F32)).astype(BF)


def kernel(amp, integ, out, raw, panel, stage, ah, al, bs, acc, part, land,
           own_sem, a2a_send, a2a_recv, stage_sem, g_send, g_recv, c_recv, rs_send, rs_recv):
    row, col = lax.axis_index("row"), lax.axis_index("col")
    core = lax.rem(row, 2)
    x = lax.rem(row // 2, 4)
    q = row // 8
    z, yhi = col // 2, lax.rem(col, 2)
    cls = lax.rem(q + yhi, 2)

    def rowid(qq, xx, kk):
        return (qq * 4 + xx) * 2 + kk

    xr, xl = lax.rem(x + 1, 4), lax.rem(x + 3, 4)
    xo = lax.rem(x + 2, 4)
    right = (rowid(q, xr, core), col)
    left = (rowid(q, xl, core), col)
    across = (rowid(1 - q, x, core), col)
    sib = (rowid(q, x, 1 - core), col)

    def a2a_dev(step):
        c = partner(step)
        return (rowid(lax.rem(cls + lax.rem(c, 2), 2), x, core), c)

    FAR_FIRST = (5, 3, 7, 1, 4, 2, 6)

    def partner(step):
        return lax.rem(z + step // 2, 4) * 2 + lax.rem(yhi + step, 2)

    def rs_dev(step):
        return (row, partner(step))

    barrier = pltpu.get_barrier_semaphore()

    def greet(dev):
        pl.semaphore_signal(barrier, inc=1, device_id=dev, device_id_type=MESH)

    for dev in (right, left, across, sib):
        greet(dev)
    for s in range(1, 8):
        greet(a2a_dev(s))
    src_slot = yhi * 4 + z

    def stage_copy(m):
        return pltpu.make_async_copy(integ.at[:, pl.ds(pl.multiple_of(m * CK, CK), CK)],
                                     stage.at[lax.rem(m, STAGES)], stage_sem.at[lax.rem(m, STAGES)])

    own_rows = pl.ds(pl.multiple_of(src_slot * 2 * TILES, 8), 2 * TILES)
    own_copy = pltpu.make_async_copy(amp.at[col], raw.at[:, own_rows], own_sem.at[0])
    own_copy.start()
    for m in range(STAGES):
        stage_copy(m).start()
    def convert(m):
        st = lax.rem(m, STAGES)
        stage_copy(m).wait()

        @pl.loop(0, AB // 16, unroll=2)
        def _(r):
            rows = pl.ds(pl.multiple_of(r * 16, 16), 16)
            hi, lo = split(stage[st, rows, :])
            ah[m, rows, :] = hi
            al[m, rows, :] = lo

        @pl.when(m + STAGES < M)
        def _():
            stage_copy(m + STAGES).start()

    pl.semaphore_wait(barrier, 11)

    for g, (m, n) in enumerate(GROUPS):
        for s in FAR_FIRST:
            pltpu.make_async_remote_copy(
                src_ref=amp.at[partner(s), pl.ds(m, n)], dst_ref=raw.at[pl.ds(m, n), own_rows],
                send_sem=a2a_send.at[0], recv_sem=a2a_recv.at[g], device_id=a2a_dev(s), device_id_type=MESH,
            ).start()

    acc[...] = jnp.zeros_like(acc)
    for m in range(PRE):
        convert(m)
    own_copy.wait()

    def slot(c, xx, kk):
        return (kk * 2 + c) * 4 + xx

    def piece(i, sl, half=None):
        rows = pl.ds(pl.multiple_of(sl * 8, 8), 8)
        if half is None:
            return panel.at[i, rows]
        return panel.at[i, rows, pl.ds(half * (CK // 2), CK // 2)]

    def send(i, sl, dev, sem, half=None):
        ref = piece(i, sl, half)
        pltpu.make_async_remote_copy(src_ref=ref, dst_ref=ref, send_sem=g_send.at[i], recv_sem=sem,
                                     device_id=dev, device_id_type=MESH).start()

    def wait(i, sl, sem):
        ref = piece(i, sl)
        pltpu.make_async_remote_copy(src_ref=ref, dst_ref=ref, send_sem=g_send.at[i], recv_sem=sem,
                                     device_id=right, device_id_type=MESH).wait_recv()

    def share(i, c):
        ref = panel.at[i, pl.ds(pl.multiple_of(slot(c, 0, core) * 8, 8), 32)]
        pltpu.make_async_remote_copy(src_ref=ref, dst_ref=ref, send_sem=g_send.at[i], recv_sem=c_recv.at[i],
                                     device_id=sib, device_id_type=MESH).start()

    own = slot(cls, x, core)

    def y_first(i):
        return (core == 0) | (lax.rem(i, EVERY) == EVERY - 1)

    def x_first(i):
        return (core == 1) & (lax.rem(i, EVERY) != EVERY - 1)

    def first(i):
        m = i
        for g, (m0, n) in enumerate(GROUPS):
            @pl.when(i == m0)
            def _():
                ref = raw.at[pl.ds(m0, n), pl.ds(0, 7 * 2 * TILES)]
                pltpu.make_async_remote_copy(src_ref=ref, dst_ref=ref, send_sem=a2a_send.at[0], recv_sem=a2a_recv.at[g],
                                             device_id=right, device_id_type=MESH).wait_recv()

        @pl.when(i < M)
        def _():
            for t in range(TILES):
                for j in range(2):
                    panel[m + j * M, pl.ds(pl.multiple_of(own * 8, 8), 8), t * 128:(t + 1) * 128] = (
                        raw[m, pl.ds(2 * t + j, 8, stride=2 * TILES), :])

        send(i, own, right, g_recv.at[i, 0])
        send(i, own, left, g_recv.at[i, 1])
        send(i, own, across, g_recv.at[i, 2])

    def from_sides(i, c, s, fwd, on_across):
        for xx, dev, k in ((xl, right, 0), (xr, left, 1)):
            wait(i, slot(c, xx, core), g_recv.at[i, s + k])
            send(i, slot(c, xx, core), dev, g_recv.at[i, fwd], k)
            if on_across:
                send(i, slot(c, xx, core), across, g_recv.at[i, 4 + k])

    def y_theirs(i):
        theirs = slot(1 - cls, x, core)
        wait(i, theirs, g_recv.at[i, 2])
        send(i, theirs, right, g_recv.at[i, 3])
        send(i, theirs, left, g_recv.at[i, 4])

    def y_sides_own(i):
        from_sides(i, cls, 0, 5, False)

    def y_sides_theirs(i):
        from_sides(i, 1 - cls, 3, 6, False)

    def y_far_own(i):
        wait(i, slot(cls, xo, core), g_recv.at[i, 5])
        share(i, cls)

    def y_far_theirs(i):
        wait(i, slot(1 - cls, xo, core), g_recv.at[i, 6])
        share(i, 1 - cls)

    def x_sides(i):
        from_sides(i, cls, 0, 3, True)

    def x_far(i):
        wait(i, slot(cls, xo, core), g_recv.at[i, 3])
        send(i, slot(cls, xo, core), across, g_recv.at[i, 6])
        share(i, cls)

    def x_theirs(i):
        for xx, k in ((x, 2), (xl, 4), (xr, 5), (xo, 6)):
            wait(i, slot(1 - cls, xx, core), g_recv.at[i, k])
        share(i, 1 - cls)

    def compute(i):
        m = lax.rem(i, M)
        ref = panel.at[i, pl.ds(0, 64)]
        pltpu.make_async_remote_copy(src_ref=ref, dst_ref=ref, send_sem=g_send.at[i], recv_sem=c_recv.at[i],
                                     device_id=sib, device_id_type=MESH).wait_recv()
        mask = lax.rem(lax.broadcasted_iota(jnp.int32, (16, CK), 0), 8) < 4
        for xx in range(4):
            v0, v1 = (jnp.concatenate([panel[i, slot(c, xx, kk) * 8:slot(c, xx, kk) * 8 + 8, :] for kk in range(2)], 0)
                      for c in range(2))
            for y, v in ((0, jnp.where(mask, v0, v1)), (1, jnp.where(mask, v1, v0))):
                hi, lo = split(v)
                at = y * 64 + xx * 16
                bs[at:at + 16, :] = hi
                bs[128 + at:128 + at + 16, :] = lo
        for a0, a1 in ((0, 704),):
            acc[a0:a1, :] += dot(ah[m, a0:a1, :], bs[...])
            acc[a0:a1, 0:128] += dot(al[m, a0:a1, :], bs[0:128, :])

    def finish(h, _):
        part[h, :, :] = (acc[:, 0:128] + acc[:, 128:256]).T
        for s in FAR_FIRST:
            c = partner(s)
            pltpu.make_async_remote_copy(
                src_ref=part.at[h, pl.ds(pl.multiple_of(c * 16, 16), 16)], dst_ref=land.at[h, col],
                send_sem=rs_send.at[h], recv_sem=rs_recv.at[h], device_id=rs_dev(s), device_id_type=MESH).start()
        land[h, col, :, :] = part[h, pl.ds(pl.multiple_of(col * 16, 16), 16), :]
        if h == 0:
            acc[...] = jnp.zeros_like(acc)

    always = lambda i: True
    work = sorted([
        (0.0, first, always), (LAG["y"], y_theirs, y_first), (LAG["xa"], y_sides_own, y_first),
        (LAG["xb"], y_sides_theirs, y_first), (LAG["oa"], y_far_own, y_first), (LAG["ob"], y_far_theirs, y_first),
        (LAG["x"], x_sides, x_first), (LAG["o"], x_far, x_first), (LAG["y3"], x_theirs, x_first),
    ], key=lambda item: item[0] % 1)
    LC = int(LAG["compute"])

    def at(step, lag, f, role):
        i = step - lag

        @pl.when((i >= 0) & (i < N) & role(i))
        def _():
            f(i)

    @pl.loop(0, N + LC)
    def _(step):
        for lag, f, role in work:
            at(step, int(lag), f, role)

        @pl.when(step < M)
        def _():
            convert(step)

        at(step, LC, compute, always)
        for h in range(2):
            at(step, LC, functools.partial(finish, h), lambda i: i == h * M + M - 1)

    for h in range(2):
        ref = land.at[h, pl.ds(0, 7)]
        pltpu.make_async_remote_copy(src_ref=ref, dst_ref=ref, send_sem=rs_send.at[h], recv_sem=rs_recv.at[h],
                                     device_id=right, device_id_type=MESH).wait_recv()
        total = land[h, 0]
        for c in range(1, 8):
            total += land[h, c]
        total = 0.5 * total
        for kk in range(2):
            for yy in range(2):
                for zz in range(4):
                    r = kk * 16 + zz * 4 + yy * 2 + h
                    s = kk * 8 + yy * 4 + zz
                    out[r:r + 1, :] = total[s:s + 1, :]

    ref = raw.at[:, pl.ds(0, 7 * 2 * TILES)]
    pltpu.make_async_remote_copy(src_ref=ref, dst_ref=ref, send_sem=a2a_send.at[0], recv_sem=a2a_recv.at[0],
                                 device_id=right, device_id_type=MESH).wait_send()

    @pl.loop(0, N)
    def _(i):
        ref = panel.at[i, pl.ds(0, 120)]
        pltpu.make_async_remote_copy(src_ref=ref, dst_ref=ref, send_sem=g_send.at[i], recv_sem=c_recv.at[i],
                                     device_id=right, device_id_type=MESH).wait_send()

    for h in range(2):
        ref = land.at[h, pl.ds(0, 7)]
        pltpu.make_async_remote_copy(src_ref=ref, dst_ref=ref, send_sem=rs_send.at[h], recv_sem=rs_recv.at[h],
                                     device_id=right, device_id_type=MESH).wait_send()


def per_device(amplitudes, integrals):
    amp = amplitudes.reshape(512, 128, 2).transpose(0, 2, 1).reshape(8, M, 2 * TILES, 128)
    dma = pltpu.SemaphoreType.DMA
    out = pl.pallas_call(
        kernel,
        out_shape=pltpu.VMEM((32, AB), F32),
        in_specs=[pl.BlockSpec(memory_space=pl.ANY)] * 2,
        out_specs=pl.BlockSpec(memory_space=pltpu.VMEM),
        scratch_shapes=[
            pltpu.VMEM((M, 8 * 2 * TILES, 128), F32),
            pltpu.VMEM((N, 128, CK), F32),
            pltpu.VMEM((STAGES, AB, CK), F32),
            pltpu.VMEM((M, AB, CK), BF),
            pltpu.VMEM((M, AB, CK), BF),
            pltpu.VMEM((256, CK), BF),
            pltpu.VMEM((AB, 256), F32),
            pltpu.VMEM((2, 128, AB), F32),
            pltpu.VMEM((2, 8, 16, AB), F32),
            dma((1,)), dma((1,)), dma((len(GROUPS),)), dma((STAGES,)),
            dma((N,)), dma((N, 7)), dma((N,)), dma((2,)), dma((2,)),
        ],
        compiler_params=pltpu.CompilerParams(collective_id=0, has_side_effects=True, vmem_limit_bytes=60 * 2**20),
        cost_estimate=pl.CostEstimate(flops=2 * AB * K * 256, bytes_accessed=4 * AB * K, transcendentals=0),
    )(amp, integrals)
    return out.T


def solution(mesh):
    return jax.shard_map(
        per_device,
        mesh=mesh,
        in_specs=(P(None, ("row", "col")), P("row", "col")),
        out_specs=P("row", "col"),
        check_vma=False,
    )
```

```python
import functools

import jax
import jax.numpy as jnp
from jax import lax
from jax.experimental import pallas as pl
from jax.experimental.pallas import tpu as pltpu
from jax.sharding import PartitionSpec as P

MESH = pl.DeviceIdType.MESH
BF = jnp.bfloat16
F32 = jnp.float32
NT = (((1,), (1,)), ((), ()))

K = 8192
AB = 704
M = 8
CK = K // M
N = 2 * M
TILES = CK // 128
GROUPS = tuple((m, 1) for m in range(M))
PRE = 0
STAGES = 6
LAG = dict(y=4.1, xa=7.2, xb=7.3, oa=10.2, ob=10.3, x=6.2, o=9.2, y3=13.3, compute=14)
EVERY = 99


def dot(a, b):
    return lax.dot_general(a, b, NT, preferred_element_type=F32)


def split(v):
    hi = v.astype(BF)
    return hi, (v - hi.astype(F32)).astype(BF)


def kernel(amp, integ, out, raw, panel, stage, ah, al, bs, acc, part, land,
           own_sem, a2a_send, a2a_recv, stage_sem, g_send, g_recv, c_recv, rs_send, rs_recv):
    row, col = lax.axis_index("row"), lax.axis_index("col")
    core = lax.rem(row, 2)
    x = lax.rem(row // 2, 4)
    q = row // 8
    z, yhi = col // 2, lax.rem(col, 2)
    cls = lax.rem(q + yhi, 2)

    def rowid(qq, xx, kk):
        return (qq * 4 + xx) * 2 + kk

    xr, xl = lax.rem(x + 1, 4), lax.rem(x + 3, 4)
    xo = lax.rem(x + 2, 4)
    right = (rowid(q, xr, core), col)
    left = (rowid(q, xl, core), col)
    across = (rowid(1 - q, x, core), col)
    sib = (rowid(q, x, 1 - core), col)

    def a2a_dev(step):
        c = partner(step)
        return (rowid(lax.rem(cls + lax.rem(c, 2), 2), x, core), c)

    FAR_FIRST = (5, 3, 7, 1, 4, 2, 6)

    def partner(step):
        return lax.rem(z + step // 2, 4) * 2 + lax.rem(yhi + step, 2)

    def rs_dev(step):
        return (row, partner(step))

    barrier = pltpu.get_barrier_semaphore()

    def greet(dev):
        pl.semaphore_signal(barrier, inc=1, device_id=dev, device_id_type=MESH)

    for dev in (right, left, across, sib):
        greet(dev)
    for s in range(1, 8):
        greet(a2a_dev(s))
    src_slot = yhi * 4 + z

    def stage_copy(m):
        return pltpu.make_async_copy(integ.at[:, pl.ds(pl.multiple_of(m * CK, CK), CK)],
                                     stage.at[lax.rem(m, STAGES)], stage_sem.at[lax.rem(m, STAGES)])

    own_rows = pl.ds(pl.multiple_of(src_slot * 2 * TILES, 8), 2 * TILES)
    own_copy = pltpu.make_async_copy(amp.at[col], raw.at[:, own_rows], own_sem.at[0])
    own_copy.start()
    for m in range(STAGES):
        stage_copy(m).start()
    def convert(m):
        st = lax.rem(m, STAGES)
        stage_copy(m).wait()

        @pl.loop(0, AB // 16, unroll=2)
        def _(r):
            rows = pl.ds(pl.multiple_of(r * 16, 16), 16)
            hi, lo = split(stage[st, rows, :])
            ah[m, rows, :] = hi
            al[m, rows, :] = lo

        @pl.when(m + STAGES < M)
        def _():
            stage_copy(m + STAGES).start()

    pl.semaphore_wait(barrier, 11)

    for g, (m, n) in enumerate(GROUPS):
        for s in FAR_FIRST:
            pltpu.make_async_remote_copy(
                src_ref=amp.at[partner(s), pl.ds(m, n)], dst_ref=raw.at[pl.ds(m, n), own_rows],
                send_sem=a2a_send.at[0], recv_sem=a2a_recv.at[g], device_id=a2a_dev(s), device_id_type=MESH,
            ).start()

    acc[...] = jnp.zeros_like(acc)
    for m in range(PRE):
        convert(m)
    own_copy.wait()

    def slot(c, xx, kk):
        return (kk * 2 + c) * 4 + xx

    def piece(i, sl, half=None):
        rows = pl.ds(pl.multiple_of(sl * 8, 8), 8)
        if half is None:
            return panel.at[i, rows]
        return panel.at[i, rows, pl.ds(half * (CK // 2), CK // 2)]

    def send(i, sl, dev, sem, half=None):
        ref = piece(i, sl, half)
        pltpu.make_async_remote_copy(src_ref=ref, dst_ref=ref, send_sem=g_send.at[i], recv_sem=sem,
                                     device_id=dev, device_id_type=MESH).start()

    def wait(i, sl, sem):
        ref = piece(i, sl)
        pltpu.make_async_remote_copy(src_ref=ref, dst_ref=ref, send_sem=g_send.at[i], recv_sem=sem,
                                     device_id=right, device_id_type=MESH).wait_recv()

    def share(i, c):
        ref = panel.at[i, pl.ds(pl.multiple_of(slot(c, 0, core) * 8, 8), 32)]
        pltpu.make_async_remote_copy(src_ref=ref, dst_ref=ref, send_sem=g_send.at[i], recv_sem=c_recv.at[i],
                                     device_id=sib, device_id_type=MESH).start()

    own = slot(cls, x, core)

    def y_first(i):
        return (core == 0) | (lax.rem(i, EVERY) == EVERY - 1)

    def x_first(i):
        return (core == 1) & (lax.rem(i, EVERY) != EVERY - 1)

    def first(i):
        m = i
        for g, (m0, n) in enumerate(GROUPS):
            @pl.when(i == m0)
            def _():
                ref = raw.at[pl.ds(m0, n), pl.ds(0, 7 * 2 * TILES)]
                pltpu.make_async_remote_copy(src_ref=ref, dst_ref=ref, send_sem=a2a_send.at[0], recv_sem=a2a_recv.at[g],
                                             device_id=right, device_id_type=MESH).wait_recv()

        @pl.when(i < M)
        def _():
            for t in range(TILES):
                for j in range(2):
                    panel[m + j * M, pl.ds(pl.multiple_of(own * 8, 8), 8), t * 128:(t + 1) * 128] = (
                        raw[m, pl.ds(2 * t + j, 8, stride=2 * TILES), :])

        send(i, own, right, g_recv.at[i, 0])
        send(i, own, left, g_recv.at[i, 1])
        send(i, own, across, g_recv.at[i, 2])

    def from_sides(i, c, s, fwd, on_across):
        for xx, dev, k in ((xl, right, 0), (xr, left, 1)):
            wait(i, slot(c, xx, core), g_recv.at[i, s + k])
            send(i, slot(c, xx, core), dev, g_recv.at[i, fwd], k)
            if on_across:
                send(i, slot(c, xx, core), across, g_recv.at[i, 4 + k])

    def y_theirs(i):
        theirs = slot(1 - cls, x, core)
        wait(i, theirs, g_recv.at[i, 2])
        send(i, theirs, right, g_recv.at[i, 3])
        send(i, theirs, left, g_recv.at[i, 4])

    def y_sides_own(i):
        from_sides(i, cls, 0, 5, False)

    def y_sides_theirs(i):
        from_sides(i, 1 - cls, 3, 6, False)

    def y_far_own(i):
        wait(i, slot(cls, xo, core), g_recv.at[i, 5])
        share(i, cls)

    def y_far_theirs(i):
        wait(i, slot(1 - cls, xo, core), g_recv.at[i, 6])
        share(i, 1 - cls)

    def x_sides(i):
        from_sides(i, cls, 0, 3, True)

    def x_far(i):
        wait(i, slot(cls, xo, core), g_recv.at[i, 3])
        send(i, slot(cls, xo, core), across, g_recv.at[i, 6])
        share(i, cls)

    def x_theirs(i):
        for xx, k in ((x, 2), (xl, 4), (xr, 5), (xo, 6)):
            wait(i, slot(1 - cls, xx, core), g_recv.at[i, k])
        share(i, 1 - cls)

    def compute(i):
        m = lax.rem(i, M)
        ref = panel.at[i, pl.ds(0, 64)]
        pltpu.make_async_remote_copy(src_ref=ref, dst_ref=ref, send_sem=g_send.at[i], recv_sem=c_recv.at[i],
                                     device_id=sib, device_id_type=MESH).wait_recv()
        mask = lax.rem(lax.broadcasted_iota(jnp.int32, (16, CK), 0), 8) < 4
        for xx in range(4):
            v0, v1 = (jnp.concatenate([panel[i, slot(c, xx, kk) * 8:slot(c, xx, kk) * 8 + 8, :] for kk in range(2)], 0)
                      for c in range(2))
            for y, v in ((0, jnp.where(mask, v0, v1)), (1, jnp.where(mask, v1, v0))):
                hi, lo = split(v)
                at = y * 64 + xx * 16
                bs[at:at + 16, :] = hi
                bs[128 + at:128 + at + 16, :] = lo
        for a0, a1 in ((0, 704),):
            acc[a0:a1, :] += dot(ah[m, a0:a1, :], bs[...])
            acc[a0:a1, 0:128] += dot(al[m, a0:a1, :], bs[0:128, :])

    def finish(h, _):
        part[h, :, :] = (acc[:, 0:128] + acc[:, 128:256]).T
        for s in FAR_FIRST:
            c = partner(s)
            pltpu.make_async_remote_copy(
                src_ref=part.at[h, pl.ds(pl.multiple_of(c * 16, 16), 16)], dst_ref=land.at[h, col],
                send_sem=rs_send.at[h], recv_sem=rs_recv.at[h], device_id=rs_dev(s), device_id_type=MESH).start()
        land[h, col, :, :] = part[h, pl.ds(pl.multiple_of(col * 16, 16), 16), :]
        if h == 0:
            acc[...] = jnp.zeros_like(acc)

    always = lambda i: True
    work = sorted([
        (0.0, first, always), (LAG["y"], y_theirs, y_first), (LAG["xa"], y_sides_own, y_first),
        (LAG["xb"], y_sides_theirs, y_first), (LAG["oa"], y_far_own, y_first), (LAG["ob"], y_far_theirs, y_first),
        (LAG["x"], x_sides, x_first), (LAG["o"], x_far, x_first), (LAG["y3"], x_theirs, x_first),
    ], key=lambda item: item[0] % 1)
    LC = int(LAG["compute"])

    def at(step, lag, f, role):
        i = step - lag

        @pl.when((i >= 0) & (i < N) & role(i))
        def _():
            f(i)

    @pl.loop(0, N + LC)
    def _(step):
        for lag, f, role in work:
            at(step, int(lag), f, role)

        @pl.when(step < M)
        def _():
            convert(step)

        at(step, LC, compute, always)
        for h in range(2):
            at(step, LC, functools.partial(finish, h), lambda i: i == h * M + M - 1)

    for h in range(2):
        ref = land.at[h, pl.ds(0, 7)]
        pltpu.make_async_remote_copy(src_ref=ref, dst_ref=ref, send_sem=rs_send.at[h], recv_sem=rs_recv.at[h],
                                     device_id=right, device_id_type=MESH).wait_recv()
        total = land[h, 0]
        for c in range(1, 8):
            total += land[h, c]
        total = 0.5 * total
        for kk in range(2):
            for yy in range(2):
                for zz in range(4):
                    r = kk * 16 + zz * 4 + yy * 2 + h
                    s = kk * 8 + yy * 4 + zz
                    out[r:r + 1, :] = total[s:s + 1, :]

    ref = raw.at[:, pl.ds(0, 7 * 2 * TILES)]
    pltpu.make_async_remote_copy(src_ref=ref, dst_ref=ref, send_sem=a2a_send.at[0], recv_sem=a2a_recv.at[0],
                                 device_id=right, device_id_type=MESH).wait_send()

    @pl.loop(0, N)
    def _(i):
        ref = panel.at[i, pl.ds(0, 120)]
        pltpu.make_async_remote_copy(src_ref=ref, dst_ref=ref, send_sem=g_send.at[i], recv_sem=c_recv.at[i],
                                     device_id=right, device_id_type=MESH).wait_send()

    for h in range(2):
        ref = land.at[h, pl.ds(0, 7)]
        pltpu.make_async_remote_copy(src_ref=ref, dst_ref=ref, send_sem=rs_send.at[h], recv_sem=rs_recv.at[h],
                                     device_id=right, device_id_type=MESH).wait_send()


def per_device(amplitudes, integrals):
    amp = amplitudes.reshape(512, 128, 2).transpose(0, 2, 1).reshape(8, M, 2 * TILES, 128)
    dma = pltpu.SemaphoreType.DMA
    out = pl.pallas_call(
        kernel,
        out_shape=pltpu.VMEM((32, AB), F32),
        in_specs=[pl.BlockSpec(memory_space=pl.ANY)] * 2,
        out_specs=pl.BlockSpec(memory_space=pltpu.VMEM),
        scratch_shapes=[
            pltpu.VMEM((M, 8 * 2 * TILES, 128), F32),
            pltpu.VMEM((N, 128, CK), F32),
            pltpu.VMEM((STAGES, AB, CK), F32),
            pltpu.VMEM((M, AB, CK), BF),
            pltpu.VMEM((M, AB, CK), BF),
            pltpu.VMEM((256, CK), BF),
            pltpu.VMEM((AB, 256), F32),
            pltpu.VMEM((2, 128, AB), F32),
            pltpu.VMEM((2, 8, 16, AB), F32),
            dma((1,)), dma((1,)), dma((len(GROUPS),)), dma((STAGES,)),
            dma((N,)), dma((N, 7)), dma((N,)), dma((2,)), dma((2,)),
        ],
        compiler_params=pltpu.CompilerParams(collective_id=0, has_side_effects=True, vmem_limit_bytes=60 * 2**20),
        cost_estimate=pl.CostEstimate(flops=2 * AB * K * 256, bytes_accessed=4 * AB * K, transcendentals=0),
    )(amp, integrals)
    return out.T


def solution(mesh):
    return jax.shard_map(
        per_device,
        mesh=mesh,
        in_specs=(P(None, ("row", "col")), P("row", "col")),
        out_specs=P("row", "col"),
        check_vma=False,
    )
```

```python
import functools

import jax
import jax.numpy as jnp
from jax import lax
from jax.experimental import pallas as pl
from jax.experimental.pallas import tpu as pltpu
from jax.sharding import PartitionSpec as P

MESH = pl.DeviceIdType.MESH
BF = jnp.bfloat16
F32 = jnp.float32
NT = (((1,), (1,)), ((), ()))

K = 8192
AB = 704
M = 8
CK = K // M
N = 2 * M
TILES = CK // 128
GROUPS = tuple((m, 1) for m in range(M))
PRE = 0
STAGES = 6
LAG = dict(y=4.1, xa=7.2, xb=7.3, oa=10.2, ob=10.3, x=6.2, o=9.2, y3=13.3, compute=14)
EVERY = 99


def dot(a, b):
    return lax.dot_general(a, b, NT, preferred_element_type=F32)


def split(v):
    hi = v.astype(BF)
    return hi, (v - hi.astype(F32)).astype(BF)


def kernel(amp, integ, out, raw, panel, stage, ah, al, bs, acc, part, land,
           own_sem, a2a_send, a2a_recv, stage_sem, g_send, g_recv, c_recv, rs_send, rs_recv):
    row, col = lax.axis_index("row"), lax.axis_index("col")
    core = lax.rem(row, 2)
    x = lax.rem(row // 2, 4)
    q = row // 8
    z, yhi = col // 2, lax.rem(col, 2)
    cls = lax.rem(q + yhi, 2)

    def rowid(qq, xx, kk):
        return (qq * 4 + xx) * 2 + kk

    xr, xl = lax.rem(x + 1, 4), lax.rem(x + 3, 4)
    xo = lax.rem(x + 2, 4)
    right = (rowid(q, xr, core), col)
    left = (rowid(q, xl, core), col)
    across = (rowid(1 - q, x, core), col)
    sib = (rowid(q, x, 1 - core), col)

    def a2a_dev(step):
        c = partner(step)
        return (rowid(lax.rem(cls + lax.rem(c, 2), 2), x, core), c)

    FAR_FIRST = (5, 3, 7, 1, 4, 2, 6)

    def partner(step):
        return lax.rem(z + step // 2, 4) * 2 + lax.rem(yhi + step, 2)

    def rs_dev(step):
        return (row, partner(step))

    barrier = pltpu.get_barrier_semaphore()

    def greet(dev):
        pl.semaphore_signal(barrier, inc=1, device_id=dev, device_id_type=MESH)

    for dev in (right, left, across, sib):
        greet(dev)
    for s in range(1, 8):
        greet(a2a_dev(s))
    src_slot = yhi * 4 + z

    def stage_copy(m):
        return pltpu.make_async_copy(integ.at[:, pl.ds(pl.multiple_of(m * CK, CK), CK)],
                                     stage.at[lax.rem(m, STAGES)], stage_sem.at[lax.rem(m, STAGES)])

    own_rows = pl.ds(pl.multiple_of(src_slot * 2 * TILES, 8), 2 * TILES)
    own_copy = pltpu.make_async_copy(amp.at[col], raw.at[:, own_rows], own_sem.at[0])
    own_copy.start()
    for m in range(STAGES):
        stage_copy(m).start()
    def convert(m):
        st = lax.rem(m, STAGES)
        stage_copy(m).wait()

        @pl.loop(0, AB // 16, unroll=2)
        def _(r):
            rows = pl.ds(pl.multiple_of(r * 16, 16), 16)
            hi, lo = split(stage[st, rows, :])
            ah[m, rows, :] = hi
            al[m, rows, :] = lo

        @pl.when(m + STAGES < M)
        def _():
            stage_copy(m + STAGES).start()

    pl.semaphore_wait(barrier, 11)

    for g, (m, n) in enumerate(GROUPS):
        for s in FAR_FIRST:
            pltpu.make_async_remote_copy(
                src_ref=amp.at[partner(s), pl.ds(m, n)], dst_ref=raw.at[pl.ds(m, n), own_rows],
                send_sem=a2a_send.at[0], recv_sem=a2a_recv.at[g], device_id=a2a_dev(s), device_id_type=MESH,
            ).start()

    acc[...] = jnp.zeros_like(acc)
    for m in range(PRE):
        convert(m)
    own_copy.wait()

    def slot(c, xx, kk):
        return (kk * 2 + c) * 4 + xx

    def piece(i, sl, half=None):
        rows = pl.ds(pl.multiple_of(sl * 8, 8), 8)
        if half is None:
            return panel.at[i, rows]
        return panel.at[i, rows, pl.ds(half * (CK // 2), CK // 2)]

    def send(i, sl, dev, sem, half=None):
        ref = piece(i, sl, half)
        pltpu.make_async_remote_copy(src_ref=ref, dst_ref=ref, send_sem=g_send.at[i], recv_sem=sem,
                                     device_id=dev, device_id_type=MESH).start()

    def wait(i, sl, sem):
        ref = piece(i, sl)
        pltpu.make_async_remote_copy(src_ref=ref, dst_ref=ref, send_sem=g_send.at[i], recv_sem=sem,
                                     device_id=right, device_id_type=MESH).wait_recv()

    def share(i, c):
        ref = panel.at[i, pl.ds(pl.multiple_of(slot(c, 0, core) * 8, 8), 32)]
        pltpu.make_async_remote_copy(src_ref=ref, dst_ref=ref, send_sem=g_send.at[i], recv_sem=c_recv.at[i],
                                     device_id=sib, device_id_type=MESH).start()

    own = slot(cls, x, core)

    def y_first(i):
        return (core == 0) | (lax.rem(i, EVERY) == EVERY - 1)

    def x_first(i):
        return (core == 1) & (lax.rem(i, EVERY) != EVERY - 1)

    def first(i):
        m = i
        for g, (m0, n) in enumerate(GROUPS):
            @pl.when(i == m0)
            def _():
                ref = raw.at[pl.ds(m0, n), pl.ds(0, 7 * 2 * TILES)]
                pltpu.make_async_remote_copy(src_ref=ref, dst_ref=ref, send_sem=a2a_send.at[0], recv_sem=a2a_recv.at[g],
                                             device_id=right, device_id_type=MESH).wait_recv()

        @pl.when(i < M)
        def _():
            for t in range(TILES):
                for j in range(2):
                    panel[m + j * M, pl.ds(pl.multiple_of(own * 8, 8), 8), t * 128:(t + 1) * 128] = (
                        raw[m, pl.ds(2 * t + j, 8, stride=2 * TILES), :])

        send(i, own, right, g_recv.at[i, 0])
        send(i, own, left, g_recv.at[i, 1])
        send(i, own, across, g_recv.at[i, 2])

    def from_sides(i, c, s, fwd, on_across):
        for xx, dev, k in ((xl, right, 0), (xr, left, 1)):
            wait(i, slot(c, xx, core), g_recv.at[i, s + k])
            send(i, slot(c, xx, core), dev, g_recv.at[i, fwd], k)
            if on_across:
                send(i, slot(c, xx, core), across, g_recv.at[i, 4 + k])

    def y_theirs(i):
        theirs = slot(1 - cls, x, core)
        wait(i, theirs, g_recv.at[i, 2])
        send(i, theirs, right, g_recv.at[i, 3])
        send(i, theirs, left, g_recv.at[i, 4])

    def y_sides_own(i):
        from_sides(i, cls, 0, 5, False)

    def y_sides_theirs(i):
        from_sides(i, 1 - cls, 3, 6, False)

    def y_far_own(i):
        wait(i, slot(cls, xo, core), g_recv.at[i, 5])
        share(i, cls)

    def y_far_theirs(i):
        wait(i, slot(1 - cls, xo, core), g_recv.at[i, 6])
        share(i, 1 - cls)

    def x_sides(i):
        from_sides(i, cls, 0, 3, True)

    def x_far(i):
        wait(i, slot(cls, xo, core), g_recv.at[i, 3])
        send(i, slot(cls, xo, core), across, g_recv.at[i, 6])
        share(i, cls)

    def x_theirs(i):
        for xx, k in ((x, 2), (xl, 4), (xr, 5), (xo, 6)):
            wait(i, slot(1 - cls, xx, core), g_recv.at[i, k])
        share(i, 1 - cls)

    def compute(i):
        m = lax.rem(i, M)
        ref = panel.at[i, pl.ds(0, 64)]
        pltpu.make_async_remote_copy(src_ref=ref, dst_ref=ref, send_sem=g_send.at[i], recv_sem=c_recv.at[i],
                                     device_id=sib, device_id_type=MESH).wait_recv()
        mask = lax.rem(lax.broadcasted_iota(jnp.int32, (16, CK), 0), 8) < 4
        for xx in range(4):
            v0, v1 = (jnp.concatenate([panel[i, slot(c, xx, kk) * 8:slot(c, xx, kk) * 8 + 8, :] for kk in range(2)], 0)
                      for c in range(2))
            for y, v in ((0, jnp.where(mask, v0, v1)), (1, jnp.where(mask, v1, v0))):
                hi, lo = split(v)
                at = y * 64 + xx * 16
                bs[at:at + 16, :] = hi
                bs[128 + at:128 + at + 16, :] = lo
        for a0, a1 in ((0, 704),):
            both = dot(ah[m, a0:a1, :], bs[...])
            acc[a0:a1, :] += both[:, 0:128] + both[:, 128:256] + dot(al[m, a0:a1, :], bs[0:128, :])

    def finish(h, _):
        part[h, :, :] = acc[...].T
        for s in FAR_FIRST:
            c = partner(s)
            pltpu.make_async_remote_copy(
                src_ref=part.at[h, pl.ds(pl.multiple_of(c * 16, 16), 16)], dst_ref=land.at[h, col],
                send_sem=rs_send.at[h], recv_sem=rs_recv.at[h], device_id=rs_dev(s), device_id_type=MESH).start()
        land[h, col, :, :] = part[h, pl.ds(pl.multiple_of(col * 16, 16), 16), :]
        if h == 0:
            acc[...] = jnp.zeros_like(acc)

    always = lambda i: True
    work = sorted([
        (0.0, first, always), (LAG["y"], y_theirs, y_first), (LAG["xa"], y_sides_own, y_first),
        (LAG["xb"], y_sides_theirs, y_first), (LAG["oa"], y_far_own, y_first), (LAG["ob"], y_far_theirs, y_first),
        (LAG["x"], x_sides, x_first), (LAG["o"], x_far, x_first), (LAG["y3"], x_theirs, x_first),
    ], key=lambda item: item[0] % 1)
    LC = int(LAG["compute"])

    def at(step, lag, f, role):
        i = step - lag

        @pl.when((i >= 0) & (i < N) & role(i))
        def _():
            f(i)

    @pl.loop(0, N + LC)
    def _(step):
        for lag, f, role in work:
            at(step, int(lag), f, role)

        @pl.when(step < M)
        def _():
            convert(step)

        at(step, LC, compute, always)
        for h in range(2):
            at(step, LC, functools.partial(finish, h), lambda i: i == h * M + M - 1)

    for h in range(2):
        ref = land.at[h, pl.ds(0, 7)]
        pltpu.make_async_remote_copy(src_ref=ref, dst_ref=ref, send_sem=rs_send.at[h], recv_sem=rs_recv.at[h],
                                     device_id=right, device_id_type=MESH).wait_recv()
        total = land[h, 0]
        for c in range(1, 8):
            total += land[h, c]
        total = 0.5 * total
        for kk in range(2):
            for yy in range(2):
                for zz in range(4):
                    r = kk * 16 + zz * 4 + yy * 2 + h
                    s = kk * 8 + yy * 4 + zz
                    out[r:r + 1, :] = total[s:s + 1, :]

    ref = raw.at[:, pl.ds(0, 7 * 2 * TILES)]
    pltpu.make_async_remote_copy(src_ref=ref, dst_ref=ref, send_sem=a2a_send.at[0], recv_sem=a2a_recv.at[0],
                                 device_id=right, device_id_type=MESH).wait_send()

    @pl.loop(0, N)
    def _(i):
        ref = panel.at[i, pl.ds(0, 120)]
        pltpu.make_async_remote_copy(src_ref=ref, dst_ref=ref, send_sem=g_send.at[i], recv_sem=c_recv.at[i],
                                     device_id=right, device_id_type=MESH).wait_send()

    for h in range(2):
        ref = land.at[h, pl.ds(0, 7)]
        pltpu.make_async_remote_copy(src_ref=ref, dst_ref=ref, send_sem=rs_send.at[h], recv_sem=rs_recv.at[h],
                                     device_id=right, device_id_type=MESH).wait_send()


def per_device(amplitudes, integrals):
    amp = amplitudes.reshape(512, 128, 2).transpose(0, 2, 1).reshape(8, M, 2 * TILES, 128)
    dma = pltpu.SemaphoreType.DMA
    out = pl.pallas_call(
        kernel,
        out_shape=pltpu.VMEM((32, AB), F32),
        in_specs=[pl.BlockSpec(memory_space=pl.ANY)] * 2,
        out_specs=pl.BlockSpec(memory_space=pltpu.VMEM),
        scratch_shapes=[
            pltpu.VMEM((M, 8 * 2 * TILES, 128), F32),
            pltpu.VMEM((N, 128, CK), F32),
            pltpu.VMEM((STAGES, AB, CK), F32),
            pltpu.VMEM((M, AB, CK), BF),
            pltpu.VMEM((M, AB, CK), BF),
            pltpu.VMEM((256, CK), BF),
            pltpu.VMEM((AB, 128), F32),
            pltpu.VMEM((2, 128, AB), F32),
            pltpu.VMEM((2, 8, 16, AB), F32),
            dma((1,)), dma((1,)), dma((len(GROUPS),)), dma((STAGES,)),
            dma((N,)), dma((N, 7)), dma((N,)), dma((2,)), dma((2,)),
        ],
        compiler_params=pltpu.CompilerParams(collective_id=0, has_side_effects=True, vmem_limit_bytes=60 * 2**20),
        cost_estimate=pl.CostEstimate(flops=2 * AB * K * 256, bytes_accessed=4 * AB * K, transcendentals=0),
    )(amp, integrals)
    return out.T


def solution(mesh):
    return jax.shard_map(
        per_device,
        mesh=mesh,
        in_specs=(P(None, ("row", "col")), P("row", "col")),
        out_specs=P("row", "col"),
        check_vma=False,
    )
```
